256 devices in a mesh: occ: 32 (over z, y), vir: 8 (over x, core).
Axes of the slice: x: 4, y: 4, z: 8, core: 2. Of those that a mesh axis runs over, the one named last changes fastest.
Arguments:
- amplitudes: bfloat16 [256, 32, 128, 128], P('occ', None, 'vir'), may hold values from -6 to 6
- integrals: bfloat16 [64, 32, 128, 128], P('occ', 'vir'), may hold values from -0.09375 to 0.09375
- tile_list: int32 [256, 32], P('occ'), may hold values from 0 to 63, as said below
- counts: int32 [256], P('occ'), may hold values from 1 to 32, 5120 in all
Outputs:
- ladder: bfloat16 [256, 32, 128, 128], P('occ', 'vir')
The draws below stay inside these ranges and needn't reach their ends.
Inputs may be any that keep to these rules, and one draw needn't show every extreme that they name: `tile_list`: within one pair block the 32 entries are distinct. Slots 0 to counts[b] - 1 of block b are live; some block has all 32 live.
All inputs are finite; a program needn't handle non-finite values.
Results may differ from the reference program's by a relative error of at most 0.001.
Values may be sent and summed in bfloat16 or wider, within the bound.
A program may use at most 128 MiB of HBM per device.

```python
import math
import jax
import jax.numpy as jnp
import numpy as np
from jax import lax

TILE = 128
PB = 128
SLOTS = 32
NBLK = 256
NCD = 64
NAB = 32


def draw_tile_list(key, part):
    key = jax.random.fold_in(key, 7)
    keys = jax.random.split(key, NBLK)
    return jax.vmap(lambda k: jax.random.permutation(k, NCD)[:SLOTS])(keys).astype(jnp.int32)


def block_scale(rng, shape, cuts, least, largest):
    level, own = 1.0, jax.random.fold_in(rng, 6)
    for axis_at, blocks in cuts:
        steps = jnp.exp(jax.random.uniform(jax.random.fold_in(own, axis_at), (blocks,), jnp.float32, least / len(cuts), largest / len(cuts)))
        level = level * jnp.repeat(steps, shape[axis_at] // blocks).reshape([-1 if axis == axis_at else 1 for axis in range(len(shape))])
    return level


def split_up(amount, total, most, lean):
    loads = [(1 << 20) // math.isqrt(rank ** lean) + 1 for rank in range(2, amount + 1)]
    surplus, given = total - most - (amount - 1), [1] * (amount - 1)
    while surplus > 0:
        free = [i for i in range(amount - 1) if given[i] < most]
        pool, budget = sum([loads[i] for i in free]), surplus
        for i in free:
            addition = min(most - given[i], max(1, budget * loads[i] // pool), surplus)
            given[i] = given[i] + addition
            surplus = surplus - addition
    return np.array([most] + given)


def ragged_sizes(own_key, amount, total, reach, lean):
    if amount == 2:
        one = jax.random.randint(own_key, (), max(1, total - reach), min(reach, total - 1) + 1)
        return jnp.stack([one, total - one])
    tallies = jnp.asarray(split_up(amount, total, reach, lean), jnp.int32)
    twos = (amount - 1) // 2
    source_of, receiver = tallies[1:1 + 2 * twos:2], tallies[2:2 + 2 * twos:2]
    margin = jnp.minimum(source_of - 1, reach - receiver)
    moved = jax.random.randint(jax.random.fold_in(own_key, 1), (twos,), 0, 1 << 20) % (margin + 1)
    tallies = tallies.at[1:1 + 2 * twos:2].set(source_of - moved).at[2:2 + 2 * twos:2].set(receiver + moved)
    return tallies[jax.random.permutation(jax.random.fold_in(own_key, 2), amount)]


def scatter_about(rng, shape, scale, bound, cuts=(), kind=jnp.bfloat16):
    level = block_scale(rng, shape, cuts, -0.22, 0.18) if cuts else 1.0
    drawn = jax.random.normal(rng, shape, jnp.float32) * scale * level
    return jnp.minimum(jnp.maximum(drawn, -bound), bound).astype(kind)


def setup_inputs(seed: int = 0) -> dict:
    key_of = jax.random.split(jax.random.key(seed), 5)
    return {
        "amplitudes": scatter_about(key_of[0], (NBLK, SLOTS, PB, TILE), 1.0, 6.0, ((0, 32), (2, 8))),
        "integrals": scatter_about(key_of[1], (NCD, NAB, TILE, TILE), (SLOTS * TILE) ** -0.5, 0.09375, ((0, 32), (1, 8))),
        "tile_list": draw_tile_list(jax.random.fold_in(key_of[4], 71), 0),
        "counts": ragged_sizes(key_of[3], NBLK, NBLK * SLOTS * 5 // 8, SLOTS, 2).astype(jnp.int32),
    }


def reference(amplitudes, integrals, tile_list, counts):
    slot_ids = jnp.arange(SLOTS, dtype=jnp.int32)

    def one_block(args):
        amp_block, listed, count = args
        picked = jnp.take(integrals, listed.astype(jnp.int32), axis=0).astype(jnp.float32)
        live = (slot_ids < count).astype(jnp.float32)
        rows = amp_block.astype(jnp.float32) * live[:, None, None]
        return jnp.einsum("spt,satu->apu", rows, picked).astype(jnp.bfloat16)

    return lax.map(one_block, (amplitudes, tile_list, counts))
```

```python
import collections
import functools
import heapq
import itertools

import jax
import jax.numpy as jnp
from jax import lax
from jax.experimental import pallas as pl
from jax.experimental.pallas import tpu as pltpu
from jax.sharding import PartitionSpec as P

MESH = pl.DeviceIdType.MESH
NX, NY, NZ = 4, 4, 8
TILE, SLOTS, NB, NA = 128, 32, 8, 4
ROWS = 2 * NA * TILE
SPLIT = 416
ROW_NS, HOP_NS, HANDLER_NS, RELAY_NS = 5.6, 2400.0, 80.0, 2500.0
QUEUE_NS = {"x": 9000.0, "y": 3500.0, "z": 3500.0}
LARGE_NS, BLOCK_NS, SMALL_NS = 170.0, 145.0, 460.0
Z_RANK, Y_RANK = (2, 0.5, -2, -2), (3, -0.5, 1, 2)
HALVES = {1: (None,), 2: (None,)}
GROUPS = (4, 2, 2)
LAST_DY = (0, 1, 3, 2)
LATE = 24
VMEM_KIB = 48 * 2**10


def part_rows(part, half):
    start, rows = (0, SPLIT) if part == 1 else (SPLIT, ROWS - SPLIT)
    if half is None:
        return start, rows
    cut = rows // 2 // 16 * 16
    return (start, cut) if half == 0 else (start + cut, rows - cut)


def group_of(block):
    first = 0
    for g, size in enumerate(GROUPS):
        if block < first + size:
            return g, block - first
        first += size


def plan():
    free, ready, heap, count = collections.defaultdict(float), collections.defaultdict(list), [], itertools.count()
    steps, now = [], 0.0
    large = [(g, dz % NZ) for dz in (0, 1, -1, 2, -2, 3, -3) for g in range(len(GROUPS))]
    small = list(LAST_DY)
    rows_left = {(dz, dy): ROWS for dz in range(NZ) for dy in range(NY)}
    rows_left[0, 0] = 0
    blocks_left, blocks_at = [4 * size for size in GROUPS], [0.0] * len(GROUPS)

    def side(direction):
        return 0 if direction > 0 else 1

    def add(part, dz, dy, half, axis, direction):
        dz, dy = (dz - direction, dy) if axis == "z" else (dz, dy - direction)
        weights = Z_RANK if axis == "z" else Y_RANK
        rank = sum(w * v for w, v in zip(weights, (abs(dz), abs(dy), part == 2, half is not None)))
        piece = ("i", part, dz, dy, half, axis, direction)
        ready[axis, direction].append((rank, next(count), part_rows(part, half)[1], piece))

    def add_block(block, stage, direction):
        rank = block if stage == 2 else NB + block
        rows = SLOTS * 16 // stage
        ready["x", direction].append((rank, next(count), rows, ("a", block, stage, direction)))

    def sends():
        out, more = [], True
        while more:
            more = False
            for link in [(axis, direction) for axis in "yzx" for direction in (1, -1)]:
                if ready[link] and free[link] - now < QUEUE_NS[link[0]]:
                    item = min(ready[link])
                    ready[link].remove(item)
                    free[link] = max(now, free[link]) + item[2] * ROW_NS
                    heapq.heappush(heap, (free[link] + HOP_NS, next(count), item[3]))
                    out.append(item[3])
                    more = True
        return out

    for direction in (1, -1):
        for part in (1, 2):
            for half in HALVES[part]:
                add(part, 0, 0, half, "y", direction)
                add(part, 0, 0, half, "z", direction)
        for block in range(NB):
            add_block(block, 1, direction)
    steps.append((None, sends()))
    while heap or small:
        while small and (not heap or heap[0][0] > now):
            able = [g for g in range(len(GROUPS)) if not blocks_left[g] and (blocks_at[g] <= now or not heap)]
            fit = [u for u in large if u[0] in able and not any(rows_left[u[1], dy] for dy in range(NY))]
            if fit:
                large.remove(fit[0])
                now = max(now, blocks_at[fit[0][0]]) + LARGE_NS + BLOCK_NS * GROUPS[fit[0][0]]
                steps.append((("large", *fit[0]), sends()))
            elif not large and not rows_left[NZ // 2, small[0]]:
                now += SMALL_NS
                steps.append((("small", small.pop(0)), sends()))
            else:
                break
        if not heap:
            continue
        at, _, piece = heapq.heappop(heap)
        now = max(now, at) + HANDLER_NS
        if piece[0] == "a":
            _, block, stage, direction = piece
            if stage == 1:
                add_block(block, 2, direction)
            g = group_of(block)[0]
            blocks_left[g] -= 1
            blocks_at[g] = now + RELAY_NS
        else:
            _, part, dz, dy, half, axis, direction = piece
            rows_left[dz % NZ, dy % NY] -= part_rows(part, half)[1]
            hops, last = (abs(dz), NZ // 2) if axis == "z" else (abs(dy), NY // 2)
            if hops < last - 1:
                add(part, dz, dy, half, axis, direction)
            elif hops == last - 1 and half in (None, side(direction)):
                add(part, dz, dy, side(direction), axis, direction)
            if (part, axis) in ((1, "y"), (2, "z")):
                for turn in (1, -1):
                    add(part, dz, dy, half, "z" if axis == "y" else "y", turn)
        steps.append((piece, sends()))
    return steps


def kernel(steps, amp, ints, tiles_hbm, counts_hbm, result, blocks0, blocks1, blocks2, pieces, lhs, total, tiles, counts, slot_v,
           slot_s, send_sem, recv_sem, relay_send, relay_recv, local_sem):
    occ, vir = lax.axis_index("occ"), lax.axis_index("vir")
    x, core, z, y = vir // 2, vir % 2, occ // NY, occ % NY
    blocks = (blocks0, blocks1, blocks2)

    def near(axis, d):
        if axis == "x":
            return {"vir": (x + d + NX) % NX * 2 + core}
        if axis == "y":
            return {"occ": z * NY + (y + d + NY) % NY}
        return {"occ": (z + d + NZ) % NZ * NY + y}

    partner = {"vir": x * 2 + 1 - core}
    barrier = pltpu.get_barrier_semaphore()
    for device in [partner] + [near(axis, d) for axis in "xyz" for d in (1, -1)]:
        pl.semaphore_signal(barrier, inc=1, device_id=device, device_id_type=MESH)
    pl.semaphore_wait(barrier, 7)

    def vir_at(d, c):
        return (x + d + NX) % NX * 2 + c

    def block_at(owner, b, half=None):
        slots = pl.ds(0, SLOTS) if half is None else pl.ds(half * (SLOTS // 2), SLOTS // 2)
        g, place = group_of(b)
        return blocks[g].at[owner, place, slots]

    def side(d):
        return 0 if d > 0 else 1

    order = [piece for _, sent in steps for piece in sent]
    number = {piece: i for i, piece in enumerate(order)}

    def copy(piece, arriving=False):
        i = number[piece]
        if piece[0] == "a":
            _, b, stage, d = piece
            axis = "x"
            if stage == 1:
                src, dst = amp.at[b], block_at(vir_at(-d, core) if arriving else vir, b)
            else:
                src = block_at(vir_at(-d, core), b, side(d))
                dst = block_at(vir_at(2, core), b, side(d)) if arriving else src
        else:
            _, part, dz, dy, half, axis, d = piece
            rows = pl.ds(*part_rows(part, half))
            oz, oy = (dz + d, dy) if axis == "z" else (dz, dy + d)
            src = ints.at[rows] if (oz, oy) == (0, 0) else pieces.at[oz % NZ, oy % NY, rows]
            dst = pieces.at[dz % NZ, dy % NY, rows]
        return pltpu.make_async_remote_copy(
            src, dst, send_sem.at[i], recv_sem.at[i], device_id=near(axis, d), device_id_type=MESH
        )

    relays = [("own", b) for b in range(NB)] + [piece for piece in order if piece[0] == "a"]
    relay_number = {piece: i for i, piece in enumerate(relays)}

    def relay(piece, arriving=False):
        i = relay_number[piece]
        c = 1 - core if arriving else core
        if piece[0] == "own":
            dst = block_at(vir_at(0, c), piece[1])
            src = amp.at[piece[1]]
        else:
            _, b, stage, d = piece
            dst = block_at(vir_at(-d, c), b) if stage == 1 else block_at(vir_at(2, c), b, side(d))
            src = dst
        return pltpu.make_async_remote_copy(
            src, dst, relay_send.at[i], relay_recv.at[i], device_id=partner, device_id_type=MESH
        )

    own_blocks = [pltpu.make_async_copy(amp.at[b], block_at(vir, b), local_sem.at[b]) for b in range(NB)]
    own_piece = pltpu.make_async_copy(ints, pieces.at[0, 0], local_sem.at[NB])

    def prepare():
        lists = [
            pltpu.make_async_copy(tiles_hbm, tiles, local_sem.at[NB + 4]),
            pltpu.make_async_copy(counts_hbm, counts, local_sem.at[NB + 5]),
        ]
        for read in lists:
            read.start()
        own_piece.start()
        for b in range(NB):
            own_blocks[b].start()
            relay(("own", b)).start()
        for read in lists:
            read.wait()
        lane = lax.broadcasted_iota(jnp.int32, (NB, 128), 1)
        row = lax.broadcasted_iota(jnp.int32, (NB, 128), 0)
        tile = 2 * ((z + lane // 8) % NZ * NY + (y + lane // 2 % 4) % NY) + lane % 2
        live = jnp.zeros((NB, 128), jnp.int32)
        for b in range(NB):
            live = jnp.where(row == b, counts[b], live)
        slot = jnp.full((NB, 128), SLOTS, jnp.int32)
        listed = tiles[...]
        for s in range(SLOTS):
            slot = jnp.where((listed[:, s : s + 1] == tile) & (live > s), s, slot)
        slot_v[...] = slot
        to_scalars = pltpu.make_async_copy(slot_v, slot_s, local_sem.at[NB + 1])
        to_scalars.start()
        for group, size in zip(blocks, GROUPS):
            group[:, :, SLOTS] = jnp.zeros((2 * NX, size, 16, TILE), jnp.bfloat16)
        total[...] = jnp.zeros_like(total)
        to_scalars.wait()

    def group_ready(g):
        for b in range(NB):
            if group_of(b)[0] == g:
                own_blocks[b].wait()
        for piece in relays:
            if group_of(piece[1])[0] == g:
                relay(piece, True).wait_recv()

    rounds, units = [[]], []
    for event, sent in steps:
        if event is not None and event[0] in ("large", "small"):
            units.append(event)
            rounds.append([])
            event = None
        rounds[-1].append((event, sent))
    large = [u[1:] for u in units if u[0] == "large"]

    def run_round(r):
        for i, (event, sent) in enumerate(rounds[r]):
            if event is not None:
                copy(event, True).wait_recv()
            for piece in sent:
                copy(piece).start()
            if event is not None and event[0] == "a":
                relay(event).start()
            if r == 0 and i == 0:
                prepare()
        if r == 0:
            own_piece.wait()
        for g in range(len(GROUPS)):
            if r == [u[0] for u in large].index(g):
                group_ready(g)

    def gather(b, dz):
        g, place = group_of(b)
        found = [slot_s[b, dz * 8 + q] for q in range(8)]
        return jnp.concatenate([blocks[g][:, place, s].reshape(TILE, TILE) for s in found], axis=1)

    def origin(dz, dy):
        return jnp.concatenate(
            [
                jnp.concatenate([pieces[dz, dy, pl.ds((j * NA + a) * TILE, TILE)] for a in range(NA)], axis=1)
                for j in range(2)
            ],
            axis=0,
        )

    def run_large(g, dz):
        mine = [b for b in range(NB) if group_of(b)[0] == g]
        left = jnp.concatenate([gather(b, dz) for b in mine], axis=0)
        right = jnp.concatenate([origin(dz, dy) for dy in range(NY)], axis=0)
        here = pl.ds(mine[0] * TILE, len(mine) * TILE)
        total[here] += jnp.dot(left, right, preferred_element_type=jnp.float32)

    @pl.loop(0, len(large))
    def _(u):
        for r in range(len(large)):
            pl.when(u == r)(functools.partial(run_round, r))
        group, dz = jnp.int32(0), jnp.int32(0)
        for r, (g, d) in enumerate(large):
            group, dz = jnp.where(u == r, g, group), jnp.where(u == r, d, dz)
        for g in range(len(GROUPS)):
            pl.when(group == g)(functools.partial(run_large, g, dz))

    for b in range(NB):
        lhs[pl.ds(b * TILE, TILE)] = gather(b, NZ // 2)
    for u in range(len(large), len(units)):
        last = u == len(units) - 1
        if last:
            for piece in order[:-LATE]:
                copy(piece).wait_send()
            for piece in relays:
                relay(piece).wait_send()
        run_round(u)
        dy = units[u][1]
        sums = total[...] + jnp.dot(
            lhs[:, 2 * dy * TILE : 2 * (dy + 1) * TILE], origin(NZ // 2, dy), preferred_element_type=jnp.float32
        )
        if not last:
            total[...] = sums
            continue
        for b in range(NB):
            for a in range(NA):
                tile = sums[b * TILE : (b + 1) * TILE, a * TILE : (a + 1) * TILE]
                result[b, a] = tile.astype(jnp.bfloat16)
    for piece in order[-LATE:]:
        copy(piece).wait_send()


def on_device(amplitudes, integrals, tile_list, counts):
    steps = plan()
    operands = (amplitudes, integrals.reshape(ROWS, TILE), tile_list, counts)
    copies = sum(len(sent) for _, sent in steps)
    return pl.pallas_call(
        functools.partial(kernel, steps),
        out_shape=pltpu.VMEM((NB, NA, TILE, TILE), jnp.bfloat16),
        in_specs=[pl.BlockSpec(memory_space=pltpu.HBM)] * 4,
        out_specs=pl.BlockSpec(memory_space=pltpu.VMEM),
        scratch_shapes=[
            *[pltpu.VMEM((2 * NX, size, SLOTS + 1, 16, TILE), jnp.bfloat16) for size in GROUPS],
            pltpu.VMEM((NZ, NY, ROWS, TILE), jnp.bfloat16),
            pltpu.VMEM((NB * TILE, 8 * TILE), jnp.bfloat16),
            pltpu.VMEM((NB * TILE, NA * TILE), jnp.float32),
            pltpu.VMEM((NB, SLOTS), jnp.int32),
            pltpu.SMEM((NB,), jnp.int32),
            pltpu.VMEM((NB, 128), jnp.int32),
            pltpu.SMEM((NB, 128), jnp.int32),
            pltpu.SemaphoreType.DMA((copies,)),
            pltpu.SemaphoreType.DMA((copies,)),
            pltpu.SemaphoreType.DMA((5 * NB,)),
            pltpu.SemaphoreType.DMA((5 * NB,)),
            pltpu.SemaphoreType.DMA((NB + 6,)),
        ],
        compiler_params=pltpu.CompilerParams(
            collective_id=0, has_side_effects=True, vmem_limit_bytes=VMEM_KIB * 2**10
        ),
    )(*[pltpu.with_memory_space_constraint(x, pltpu.HBM) for x in operands])


def solution(mesh):
    placed = (P("occ", None, "vir", None), P("occ", "vir", None, None), P("occ", None), P("occ"))
    return jax.shard_map(
        on_device,
        mesh=mesh,
        in_specs=placed,
        out_specs=P("occ", "vir", None, None),
        check_vma=False,
    )
```

```python
import collections
import functools
import heapq
import itertools

import jax
import jax.numpy as jnp
from jax import lax
from jax.experimental import pallas as pl
from jax.experimental.pallas import tpu as pltpu
from jax.sharding import PartitionSpec as P

MESH = pl.DeviceIdType.MESH
NX, NY, NZ = 4, 4, 8
TILE, SLOTS, NB, NA = 128, 32, 8, 4
ROWS = 2 * NA * TILE
SPLIT = 416
ROW_NS, HOP_NS, HANDLER_NS, RELAY_NS = 5.6, 2400.0, 80.0, 1500.0
QUEUE_NS = {"x": 9000.0, "y": 3500.0, "z": 3500.0}
LARGE_NS, BLOCK_NS, SMALL_NS = 170.0, 145.0, 460.0
Z_RANK, Y_RANK = (2, 0.5, -2, -2), (3, -0.5, 1, 2)
HALVES = {1: (None,), 2: (None,)}
GROUPS = (4, 2, 2)
EARLY, LATER = (0, 1, -1, 2, -2), (3, -3, 4)
LATE = 24
VMEM_KIB = 48 * 2**10


def part_rows(part, half):
    start, rows = (0, SPLIT) if part == 1 else (SPLIT, ROWS - SPLIT)
    if half is None:
        return start, rows
    cut = rows // 2 // 16 * 16
    return (start, cut) if half == 0 else (start + cut, rows - cut)


def group_of(block):
    first = 0
    for g, size in enumerate(GROUPS):
        if block < first + size:
            return g, block - first
        first += size


def plan():
    free, ready, heap, count = collections.defaultdict(float), collections.defaultdict(list), [], itertools.count()
    steps, now = [], 0.0
    large = [(g, dz % NZ) for dz in EARLY for g in range(len(GROUPS))]
    small = [(dz % NZ, dy) for dz in LATER for dy in (0, 1, 3, 2)]
    rows_left = {(dz, dy): ROWS for dz in range(NZ) for dy in range(NY)}
    rows_left[0, 0] = 0
    blocks_left, blocks_at = [4 * size for size in GROUPS], [0.0] * len(GROUPS)

    def side(direction):
        return 0 if direction > 0 else 1

    def add(part, dz, dy, half, axis, direction):
        dz, dy = (dz - direction, dy) if axis == "z" else (dz, dy - direction)
        weights = Z_RANK if axis == "z" else Y_RANK
        rank = sum(w * v for w, v in zip(weights, (abs(dz), abs(dy), part == 2, half is not None)))
        piece = ("i", part, dz, dy, half, axis, direction)
        ready[axis, direction].append((rank, next(count), part_rows(part, half)[1], piece))

    def add_block(block, stage, direction):
        rank = block if stage == 2 else NB + block
        rows = SLOTS * 16 // stage
        ready["x", direction].append((rank, next(count), rows, ("a", block, stage, direction)))

    def sends():
        out, more = [], True
        while more:
            more = False
            for link in [(axis, direction) for axis in "yzx" for direction in (1, -1)]:
                if ready[link] and free[link] - now < QUEUE_NS[link[0]]:
                    item = min(ready[link])
                    ready[link].remove(item)
                    free[link] = max(now, free[link]) + item[2] * ROW_NS
                    heapq.heappush(heap, (free[link] + HOP_NS, next(count), item[3]))
                    out.append(item[3])
                    more = True
        return out

    for direction in (1, -1):
        for part in (1, 2):
            for half in HALVES[part]:
                add(part, 0, 0, half, "y", direction)
                add(part, 0, 0, half, "z", direction)
        for block in range(NB):
            add_block(block, 1, direction)
    steps.append((None, sends()))
    while heap or small:
        while small and (not heap or heap[0][0] > now):
            able = [g for g in range(len(GROUPS)) if not blocks_left[g] and (blocks_at[g] <= now or not heap)]
            fit = [u for u in large if u[0] in able and not any(rows_left[u[1], dy] for dy in range(NY))]
            if fit:
                large.remove(fit[0])
                now = max(now, blocks_at[fit[0][0]]) + LARGE_NS + BLOCK_NS * GROUPS[fit[0][0]]
                steps.append((("large", *fit[0]), sends()))
                continue
            fit = [u for u in small if len(able) == len(GROUPS) and not rows_left[u]]
            if not fit:
                break
            small.remove(fit[0])
            now += SMALL_NS
            steps.append((("small", *fit[0]), sends()))
        if not heap:
            continue
        at, _, piece = heapq.heappop(heap)
        now = max(now, at) + HANDLER_NS
        if piece[0] == "a":
            _, block, stage, direction = piece
            if stage == 1:
                add_block(block, 2, direction)
            g = group_of(block)[0]
            blocks_left[g] -= 1
            blocks_at[g] = now + RELAY_NS
        else:
            _, part, dz, dy, half, axis, direction = piece
            rows_left[dz % NZ, dy % NY] -= part_rows(part, half)[1]
            hops, last = (abs(dz), NZ // 2) if axis == "z" else (abs(dy), NY // 2)
            if hops < last - 1:
                add(part, dz, dy, half, axis, direction)
            elif hops == last - 1 and half in (None, side(direction)):
                add(part, dz, dy, side(direction), axis, direction)
            if (part, axis) in ((1, "y"), (2, "z")):
                for turn in (1, -1):
                    add(part, dz, dy, half, "z" if axis == "y" else "y", turn)
        steps.append((piece, sends()))
    return steps


def kernel(steps, amp, ints, tiles_hbm, counts_hbm, result, blocks0, blocks1, blocks2, pieces, total, tiles, counts, slot_v,
           slot_s, send_sem, recv_sem, relay_send, relay_recv, local_sem):
    occ, vir = lax.axis_index("occ"), lax.axis_index("vir")
    x, core, z, y = vir // 2, vir % 2, occ // NY, occ % NY
    blocks = (blocks0, blocks1, blocks2)

    def near(axis, d):
        if axis == "x":
            return {"vir": (x + d + NX) % NX * 2 + core}
        if axis == "y":
            return {"occ": z * NY + (y + d + NY) % NY}
        return {"occ": (z + d + NZ) % NZ * NY + y}

    partner = {"vir": x * 2 + 1 - core}
    barrier = pltpu.get_barrier_semaphore()
    for device in [partner] + [near(axis, d) for axis in "xyz" for d in (1, -1)]:
        pl.semaphore_signal(barrier, inc=1, device_id=device, device_id_type=MESH)
    pl.semaphore_wait(barrier, 7)

    def vir_at(d, c):
        return (x + d + NX) % NX * 2 + c

    def block_at(owner, b, half=None):
        slots = pl.ds(0, SLOTS) if half is None else pl.ds(half * (SLOTS // 2), SLOTS // 2)
        g, place = group_of(b)
        return blocks[g].at[owner, place, slots]

    def side(d):
        return 0 if d > 0 else 1

    order = [piece for _, sent in steps for piece in sent]
    number = {piece: i for i, piece in enumerate(order)}

    def copy(piece, arriving=False):
        i = number[piece]
        if piece[0] == "a":
            _, b, stage, d = piece
            axis = "x"
            if stage == 1:
                src, dst = amp.at[b], block_at(vir_at(-d, core) if arriving else vir, b)
            else:
                src = block_at(vir_at(-d, core), b, side(d))
                dst = block_at(vir_at(2, core), b, side(d)) if arriving else src
        else:
            _, part, dz, dy, half, axis, d = piece
            rows = pl.ds(*part_rows(part, half))
            oz, oy = (dz + d, dy) if axis == "z" else (dz, dy + d)
            src = ints.at[rows] if (oz, oy) == (0, 0) else pieces.at[oz % NZ, oy % NY, rows]
            dst = pieces.at[dz % NZ, dy % NY, rows]
        return pltpu.make_async_remote_copy(
            src, dst, send_sem.at[i], recv_sem.at[i], device_id=near(axis, d), device_id_type=MESH
        )

    relays = [("own", b) for b in range(NB)] + [piece for piece in order if piece[0] == "a"]
    relay_number = {piece: i for i, piece in enumerate(relays)}

    def relay(piece, arriving=False):
        i = relay_number[piece]
        c = 1 - core if arriving else core
        if piece[0] == "own":
            dst = block_at(vir_at(0, c), piece[1])
            src = amp.at[piece[1]]
        else:
            _, b, stage, d = piece
            dst = block_at(vir_at(-d, c), b) if stage == 1 else block_at(vir_at(2, c), b, side(d))
            src = dst
        return pltpu.make_async_remote_copy(
            src, dst, relay_send.at[i], relay_recv.at[i], device_id=partner, device_id_type=MESH
        )

    own_blocks = [pltpu.make_async_copy(amp.at[b], block_at(vir, b), local_sem.at[b]) for b in range(NB)]
    own_piece = pltpu.make_async_copy(ints, pieces.at[0, 0], local_sem.at[NB])

    def prepare():
        lists = [
            pltpu.make_async_copy(tiles_hbm, tiles, local_sem.at[NB + 4]),
            pltpu.make_async_copy(counts_hbm, counts, local_sem.at[NB + 5]),
        ]
        for read in lists:
            read.start()
        own_piece.start()
        for b in range(NB):
            own_blocks[b].start()
            relay(("own", b)).start()
        for read in lists:
            read.wait()
        lane = lax.broadcasted_iota(jnp.int32, (NB, 128), 1)
        row = lax.broadcasted_iota(jnp.int32, (NB, 128), 0)
        tile = 2 * ((z + lane // 8) % NZ * NY + (y + lane // 2 % 4) % NY) + lane % 2
        live = jnp.zeros((NB, 128), jnp.int32)
        for b in range(NB):
            live = jnp.where(row == b, counts[b], live)
        slot = jnp.full((NB, 128), SLOTS, jnp.int32)
        listed = tiles[...]
        for s in range(SLOTS):
            slot = jnp.where((listed[:, s : s + 1] == tile) & (live > s), s, slot)
        slot_v[...] = slot
        to_scalars = pltpu.make_async_copy(slot_v, slot_s, local_sem.at[NB + 1])
        to_scalars.start()
        for group, size in zip(blocks, GROUPS):
            group[:, :, SLOTS] = jnp.zeros((2 * NX, size, 16, TILE), jnp.bfloat16)
        total[...] = jnp.zeros_like(total)
        to_scalars.wait()

    def group_ready(g):
        for b in range(NB):
            if group_of(b)[0] == g:
                own_blocks[b].wait()
        for piece in relays:
            if group_of(piece[1])[0] == g:
                relay(piece, True).wait_recv()

    rounds, units = [[]], []
    for event, sent in steps:
        if event is not None and event[0] in ("large", "small"):
            units.append(event)
            rounds.append([])
            event = None
        rounds[-1].append((event, sent))
    first_use = [[u[:2] for u in units].index(("large", g)) for g in range(len(GROUPS))]

    def run_round(r):
        for i, (event, sent) in enumerate(rounds[r]):
            if event is not None:
                copy(event, True).wait_recv()
            for piece in sent:
                copy(piece).start()
            if event is not None and event[0] == "a":
                relay(event).start()
            if r == 0 and i == 0:
                prepare()
        if r == 0:
            own_piece.wait()
        for g in range(len(GROUPS)):
            if r == first_use[g]:
                group_ready(g)

    def gather(b, dz, tiles):
        g, place = group_of(b)
        found = [slot_s[b, dz * 8 + q] for q in tiles]
        return jnp.concatenate([blocks[g][:, place, s].reshape(TILE, TILE) for s in found], axis=1)

    def origin(dz, dy):
        return jnp.concatenate(
            [
                jnp.concatenate([pieces[dz, dy, pl.ds((j * NA + a) * TILE, TILE)] for a in range(NA)], axis=1)
                for j in range(2)
            ],
            axis=0,
        )

    def run_large(g, dz):
        mine = [b for b in range(NB) if group_of(b)[0] == g]
        left = jnp.concatenate([gather(b, dz, range(8)) for b in mine], axis=0)
        right = jnp.concatenate([origin(dz, dy) for dy in range(NY)], axis=0)
        here = pl.ds(mine[0] * TILE, len(mine) * TILE)
        total[here] += jnp.dot(left, right, preferred_element_type=jnp.float32)

    def run_small(dz, dy):
        left = jnp.concatenate([gather(b, dz, (2 * dy, 2 * dy + 1)) for b in range(NB)], axis=0)
        return total[...] + jnp.dot(left, origin(dz, dy), preferred_element_type=jnp.float32)

    def run_units(first, stop):
        @pl.loop(first, stop)
        def _(u):
            dz = jnp.int32(0)
            for r in range(first, stop):
                pl.when(u == r)(functools.partial(run_round, r))
                dz = jnp.where(u == r, units[r][2], dz)
            run_large(units[first][1], dz)

    u = 0
    while u < len(units) - 1:
        if units[u][0] == "small":
            run_round(u)
            total[...] = run_small(*units[u][1:])
            u += 1
            continue
        stop = u + 1
        while units[stop][:2] == units[u][:2]:
            stop += 1
        run_units(u, stop)
        u = stop

    for piece in order[:-LATE]:
        copy(piece).wait_send()
    for piece in relays:
        relay(piece).wait_send()
    run_round(len(units) - 1)
    sums = run_small(*units[-1][1:])
    for b in range(NB):
        for a in range(NA):
            result[b, a] = sums[b * TILE : (b + 1) * TILE, a * TILE : (a + 1) * TILE].astype(jnp.bfloat16)
    for piece in order[-LATE:]:
        copy(piece).wait_send()


def on_device(amplitudes, integrals, tile_list, counts):
    steps = plan()
    operands = (amplitudes, integrals.reshape(ROWS, TILE), tile_list, counts)
    copies = sum(len(sent) for _, sent in steps)
    return pl.pallas_call(
        functools.partial(kernel, steps),
        out_shape=pltpu.VMEM((NB, NA, TILE, TILE), jnp.bfloat16),
        in_specs=[pl.BlockSpec(memory_space=pltpu.HBM)] * 4,
        out_specs=pl.BlockSpec(memory_space=pltpu.VMEM),
        scratch_shapes=[
            *[pltpu.VMEM((2 * NX, size, SLOTS + 1, 16, TILE), jnp.bfloat16) for size in GROUPS],
            pltpu.VMEM((NZ, NY, ROWS, TILE), jnp.bfloat16),
            pltpu.VMEM((NB * TILE, NA * TILE), jnp.float32),
            pltpu.VMEM((NB, SLOTS), jnp.int32),
            pltpu.SMEM((NB,), jnp.int32),
            pltpu.VMEM((NB, 128), jnp.int32),
            pltpu.SMEM((NB, 128), jnp.int32),
            pltpu.SemaphoreType.DMA((copies,)),
            pltpu.SemaphoreType.DMA((copies,)),
            pltpu.SemaphoreType.DMA((5 * NB,)),
            pltpu.SemaphoreType.DMA((5 * NB,)),
            pltpu.SemaphoreType.DMA((NB + 6,)),
        ],
        compiler_params=pltpu.CompilerParams(
            collective_id=0, has_side_effects=True, vmem_limit_bytes=VMEM_KIB * 2**10
        ),
    )(*[pltpu.with_memory_space_constraint(x, pltpu.HBM) for x in operands])


def solution(mesh):
    placed = (P("occ", None, "vir", None), P("occ", "vir", None, None), P("occ", None), P("occ"))
    return jax.shard_map(
        on_device,
        mesh=mesh,
        in_specs=placed,
        out_specs=P("occ", "vir", None, None),
        check_vma=False,
    )
```

```python
import collections
import functools
import heapq
import itertools

import jax
import jax.numpy as jnp
from jax import lax
from jax.experimental import pallas as pl
from jax.experimental.pallas import tpu as pltpu
from jax.sharding import PartitionSpec as P

MESH = pl.DeviceIdType.MESH
NX, NY, NZ = 4, 4, 8
TILE, SLOTS, NB, NA = 128, 32, 8, 4
ROWS = 2 * NA * TILE
SPLIT = 416
ROW_NS, HOP_NS, HANDLER_NS, RELAY_NS = 5.6, 1900.0, 80.0, 1500.0
QUEUE_NS = {"x": 5500.0, "y": 3500.0, "z": 4500.0}
LARGE_NS, BLOCK_NS, SMALL_NS, PAIR_NS, SINGLE_NS = 170.0, 145.0, 460.0, 740.0, 0.0
Z_RANK, Y_RANK = (2, 0.5, -2, 0), (0.5, -0.5, 1, -1)
HALVES = {1: (None,), 2: (None,)}
GROUPS = (4, 2, 2)
EARLY, LATER = (0, 1, -1, 2, -2), (3, -3, 4)
TOGETHER = 2
LATE = 24
VMEM_KIB = 48 * 2**10


def part_rows(part, half):
    start, rows = (0, SPLIT) if part == 1 else (SPLIT, ROWS - SPLIT)
    if half is None:
        return start, rows
    cut = rows // 2 // 16 * 16
    return (start, cut) if half == 0 else (start + cut, rows - cut)


def group_of(block):
    first = 0
    for g, size in enumerate(GROUPS):
        if block < first + size:
            return g, block - first
        first += size


def plan():
    free, ready, heap, count = collections.defaultdict(float), collections.defaultdict(list), [], itertools.count()
    steps, now = [], 0.0
    large = [(g, dz % NZ) for dz in EARLY for g in range(len(GROUPS))]
    small = [(dz % NZ, dy) for dz in LATER for dy in (0, 1, 3, 2)]
    rows_left = {(dz, dy): ROWS for dz in range(NZ) for dy in range(NY)}
    rows_left[0, 0] = 0
    blocks_left, blocks_at = [4 * size for size in GROUPS], [0.0] * len(GROUPS)

    def side(direction):
        return 0 if direction > 0 else 1

    def add(part, dz, dy, half, axis, direction):
        dz, dy = (dz - direction, dy) if axis == "z" else (dz, dy - direction)
        weights = Z_RANK if axis == "z" else Y_RANK
        rank = sum(w * v for w, v in zip(weights, (abs(dz), abs(dy), part == 2, half is not None)))
        piece = ("i", part, dz, dy, half, axis, direction)
        ready[axis, direction].append((rank, next(count), part_rows(part, half)[1], piece))

    def add_block(block, stage, direction):
        rank = block if stage == 2 else NB + block
        rows = SLOTS * 16 // stage
        ready["x", direction].append((rank, next(count), rows, ("a", block, stage, direction)))

    def sends():
        out, more = [], True
        while more:
            more = False
            for link in [(axis, direction) for axis in "yzx" for direction in (1, -1)]:
                if ready[link] and free[link] - now < QUEUE_NS[link[0]]:
                    item = min(ready[link])
                    ready[link].remove(item)
                    free[link] = max(now, free[link]) + item[2] * ROW_NS
                    heapq.heappush(heap, (free[link] + HOP_NS, next(count), item[3]))
                    out.append(item[3])
                    more = True
        return out

    for direction in (1, -1):
        for part in (1, 2):
            for half in HALVES[part]:
                add(part, 0, 0, half, "y", direction)
                add(part, 0, 0, half, "z", direction)
        for block in range(NB):
            add_block(block, 1, direction)
    steps.append((None, sends()))
    while heap or small:
        while small and (not heap or heap[0][0] > now):
            able = [g for g in range(len(GROUPS)) if not blocks_left[g] and (blocks_at[g] <= now or not heap)]
            fit = [u for u in large if u[0] in able and not any(rows_left[u[1], dy] for dy in range(NY))]
            if fit:
                large.remove(fit[0])
                now = max(now, blocks_at[fit[0][0]]) + LARGE_NS + BLOCK_NS * GROUPS[fit[0][0]]
                steps.append((("large", *fit[0]), sends()))
                continue
            fit = [u for u in small if len(able) == len(GROUPS) and not rows_left[u]]
            if not fit:
                break
            if len(fit) == 1 and len(small) > 1 and heap and heap[0][0] < now + SINGLE_NS:
                break
            fit = fit[:TOGETHER]
            small = [u for u in small if u not in fit]
            now += SMALL_NS if len(fit) == 1 else PAIR_NS
            steps.append((("small", *fit), sends()))
        if not heap:
            continue
        at, _, piece = heapq.heappop(heap)
        now = max(now, at) + HANDLER_NS
        if piece[0] == "a":
            _, block, stage, direction = piece
            if stage == 1:
                add_block(block, 2, direction)
            g = group_of(block)[0]
            blocks_left[g] -= 1
            blocks_at[g] = now + RELAY_NS
        else:
            _, part, dz, dy, half, axis, direction = piece
            rows_left[dz % NZ, dy % NY] -= part_rows(part, half)[1]
            hops, last = (abs(dz), NZ // 2) if axis == "z" else (abs(dy), NY // 2)
            if hops < last - 1:
                add(part, dz, dy, half, axis, direction)
            elif hops == last - 1 and half in (None, side(direction)):
                add(part, dz, dy, side(direction), axis, direction)
            if (part, axis) in ((1, "y"), (2, "z")):
                for turn in (1, -1):
                    add(part, dz, dy, half, "z" if axis == "y" else "y", turn)
        steps.append((piece, sends()))
    return steps


def kernel(steps, amp, ints, tiles_hbm, counts_hbm, result, blocks0, blocks1, blocks2, pieces, total, tiles, counts, slot_v,
           slot_s, send_sem, recv_sem, relay_send, relay_recv, local_sem):
    occ, vir = lax.axis_index("occ"), lax.axis_index("vir")
    x, core, z, y = vir // 2, vir % 2, occ // NY, occ % NY
    blocks = (blocks0, blocks1, blocks2)

    def near(axis, d):
        if axis == "x":
            return {"vir": (x + d + NX) % NX * 2 + core}
        if axis == "y":
            return {"occ": z * NY + (y + d + NY) % NY}
        return {"occ": (z + d + NZ) % NZ * NY + y}

    partner = {"vir": x * 2 + 1 - core}
    barrier = pltpu.get_barrier_semaphore()
    for device in [near(axis, d) for axis in "zyx" for d in (1, -1)] + [partner]:
        pl.semaphore_signal(barrier, inc=1, device_id=device, device_id_type=MESH)
    pl.semaphore_wait(barrier, 7)

    def vir_at(d, c):
        return (x + d + NX) % NX * 2 + c

    def block_at(owner, b, half=None):
        slots = pl.ds(0, SLOTS) if half is None else pl.ds(half * (SLOTS // 2), SLOTS // 2)
        g, place = group_of(b)
        return blocks[g].at[owner, place, slots]

    def side(d):
        return 0 if d > 0 else 1

    order = [piece for _, sent in steps for piece in sent]
    number = {piece: i for i, piece in enumerate(order)}

    def copy(piece, arriving=False):
        i = number[piece]
        if piece[0] == "a":
            _, b, stage, d = piece
            axis = "x"
            if stage == 1:
                src, dst = amp.at[b], block_at(vir_at(-d, core) if arriving else vir, b)
            else:
                src = block_at(vir_at(-d, core), b, side(d))
                dst = block_at(vir_at(2, core), b, side(d)) if arriving else src
        else:
            _, part, dz, dy, half, axis, d = piece
            rows = pl.ds(*part_rows(part, half))
            oz, oy = (dz + d, dy) if axis == "z" else (dz, dy + d)
            src = ints.at[rows] if (oz, oy) == (0, 0) else pieces.at[oz % NZ, oy % NY, rows]
            dst = pieces.at[dz % NZ, dy % NY, rows]
        return pltpu.make_async_remote_copy(
            src, dst, send_sem.at[i], recv_sem.at[i], device_id=near(axis, d), device_id_type=MESH
        )

    relays = [("own", b) for b in range(NB)] + [piece for piece in order if piece[0] == "a"]
    relay_number = {piece: i for i, piece in enumerate(relays)}

    def relay(piece, arriving=False):
        i = relay_number[piece]
        c = 1 - core if arriving else core
        if piece[0] == "own":
            dst = block_at(vir_at(0, c), piece[1])
            src = amp.at[piece[1]]
        else:
            _, b, stage, d = piece
            dst = block_at(vir_at(-d, c), b) if stage == 1 else block_at(vir_at(2, c), b, side(d))
            src = dst
        return pltpu.make_async_remote_copy(
            src, dst, relay_send.at[i], relay_recv.at[i], device_id=partner, device_id_type=MESH
        )

    own_blocks = [pltpu.make_async_copy(amp.at[b], block_at(vir, b), local_sem.at[b]) for b in range(NB)]
    own_piece = pltpu.make_async_copy(ints, pieces.at[0, 0], local_sem.at[NB])

    def prepare():
        lists = [
            pltpu.make_async_copy(tiles_hbm, tiles, local_sem.at[NB + 4]),
            pltpu.make_async_copy(counts_hbm, counts, local_sem.at[NB + 5]),
        ]
        for read in lists:
            read.start()
        own_piece.start()
        for b in range(NB):
            own_blocks[b].start()
            relay(("own", b)).start()
        for read in lists:
            read.wait()
        lane = lax.broadcasted_iota(jnp.int32, (NB, 128), 1)
        row = lax.broadcasted_iota(jnp.int32, (NB, 128), 0)
        tile = 2 * ((z + lane // 8) % NZ * NY + (y + lane // 2 % 4) % NY) + lane % 2
        live = jnp.zeros((NB, 128), jnp.int32)
        for b in range(NB):
            live = jnp.where(row == b, counts[b], live)
        slot = jnp.full((NB, 128), SLOTS, jnp.int32)
        listed = tiles[...]
        for s in range(SLOTS):
            slot = jnp.where((listed[:, s : s + 1] == tile) & (live > s), s, slot)
        slot_v[...] = slot
        to_scalars = pltpu.make_async_copy(slot_v, slot_s, local_sem.at[NB + 1])
        to_scalars.start()
        for group, size in zip(blocks, GROUPS):
            group[:, :, SLOTS] = jnp.zeros((2 * NX, size, 16, TILE), jnp.bfloat16)
        total[...] = jnp.zeros_like(total)
        to_scalars.wait()

    def group_ready(g):
        for b in range(NB):
            if group_of(b)[0] == g:
                own_blocks[b].wait()
        for piece in relays:
            if group_of(piece[1])[0] == g:
                relay(piece, True).wait_recv()

    rounds, units = [[]], []
    for event, sent in steps:
        if event is not None and event[0] in ("large", "small"):
            units.append(event)
            rounds.append([])
            event = None
        rounds[-1].append((event, sent))
    first_use = [[u[:2] for u in units].index(("large", g)) for g in range(len(GROUPS))]

    def run_round(r):
        for i, (event, sent) in enumerate(rounds[r]):
            if event is not None:
                copy(event, True).wait_recv()
            for piece in sent:
                copy(piece).start()
            if event is not None and event[0] == "a":
                relay(event).start()
            if r == 0 and i == 0:
                prepare()
        if r == 0:
            own_piece.wait()
        for g in range(len(GROUPS)):
            if r == first_use[g]:
                group_ready(g)

    def gather(b, dz, tiles):
        g, place = group_of(b)
        found = [slot_s[b, dz * 8 + q] for q in tiles]
        return jnp.concatenate([blocks[g][:, place, s].reshape(TILE, TILE) for s in found], axis=1)

    def origin(dz, dy):
        return jnp.concatenate(
            [
                jnp.concatenate([pieces[dz, dy, pl.ds((j * NA + a) * TILE, TILE)] for a in range(NA)], axis=1)
                for j in range(2)
            ],
            axis=0,
        )

    def run_large(g, dz):
        mine = [b for b in range(NB) if group_of(b)[0] == g]
        left = jnp.concatenate([gather(b, dz, range(8)) for b in mine], axis=0)
        right = jnp.concatenate([origin(dz, dy) for dy in range(NY)], axis=0)
        here = pl.ds(mine[0] * TILE, len(mine) * TILE)
        total[here] += jnp.dot(left, right, preferred_element_type=jnp.float32)

    def run_small(*origins):
        left = jnp.concatenate(
            [
                jnp.concatenate([gather(b, dz, (2 * dy, 2 * dy + 1)) for b in range(NB)], axis=0)
                for dz, dy in origins
            ],
            axis=1,
        )
        right = jnp.concatenate([origin(dz, dy) for dz, dy in origins], axis=0)
        return total[...] + jnp.dot(left, right, preferred_element_type=jnp.float32)

    def run_units(first, stop):
        @pl.loop(first, stop)
        def _(u):
            dz = jnp.int32(0)
            for r in range(first, stop):
                pl.when(u == r)(functools.partial(run_round, r))
                dz = jnp.where(u == r, units[r][2], dz)
            run_large(units[first][1], dz)

    u = 0
    while u < len(units) - 1:
        if units[u][0] == "small":
            run_round(u)
            total[...] = run_small(*units[u][1:])
            u += 1
            continue
        stop = u + 1
        while units[stop][:2] == units[u][:2]:
            stop += 1
        run_units(u, stop)
        u = stop

    for piece in order[:-LATE]:
        copy(piece).wait_send()
    for piece in relays:
        relay(piece).wait_send()
    run_round(len(units) - 1)
    sums = run_small(*units[-1][1:])
    for b in range(NB):
        for a in range(NA):
            result[b, a] = sums[b * TILE : (b + 1) * TILE, a * TILE : (a + 1) * TILE].astype(jnp.bfloat16)
    for piece in order[-LATE:]:
        copy(piece).wait_send()


def on_device(amplitudes, integrals, tile_list, counts):
    steps = plan()
    operands = (amplitudes, integrals.reshape(ROWS, TILE), tile_list, counts)
    copies = sum(len(sent) for _, sent in steps)
    return pl.pallas_call(
        functools.partial(kernel, steps),
        out_shape=pltpu.VMEM((NB, NA, TILE, TILE), jnp.bfloat16),
        in_specs=[pl.BlockSpec(memory_space=pltpu.HBM)] * 4,
        out_specs=pl.BlockSpec(memory_space=pltpu.VMEM),
        scratch_shapes=[
            *[pltpu.VMEM((2 * NX, size, SLOTS + 1, 16, TILE), jnp.bfloat16) for size in GROUPS],
            pltpu.VMEM((NZ, NY, ROWS, TILE), jnp.bfloat16),
            pltpu.VMEM((NB * TILE, NA * TILE), jnp.float32),
            pltpu.VMEM((NB, SLOTS), jnp.int32),
            pltpu.SMEM((NB,), jnp.int32),
            pltpu.VMEM((NB, 128), jnp.int32),
            pltpu.SMEM((NB, 128), jnp.int32),
            pltpu.SemaphoreType.DMA((copies,)),
            pltpu.SemaphoreType.DMA((copies,)),
            pltpu.SemaphoreType.DMA((5 * NB,)),
            pltpu.SemaphoreType.DMA((5 * NB,)),
            pltpu.SemaphoreType.DMA((NB + 6,)),
        ],
        compiler_params=pltpu.CompilerParams(
            collective_id=0, has_side_effects=True, vmem_limit_bytes=VMEM_KIB * 2**10
        ),
    )(*[pltpu.with_memory_space_constraint(x, pltpu.HBM) for x in operands])


def solution(mesh):
    placed = (P("occ", None, "vir", None), P("occ", "vir", None, None), P("occ", None), P("occ"))
    return jax.shard_map(
        on_device,
        mesh=mesh,
        in_specs=placed,
        out_specs=P("occ", "vir", None, None),
        check_vma=False,
    )
```

```python
import collections
import functools
import heapq
import itertools

import jax
import jax.numpy as jnp
from jax import lax
from jax.experimental import pallas as pl
from jax.experimental.pallas import tpu as pltpu
from jax.sharding import PartitionSpec as P

MESH = pl.DeviceIdType.MESH
NX, NY, NZ = 4, 4, 8
TILE, SLOTS, NB, NA = 128, 32, 8, 4
ROWS = 2 * NA * TILE
SPLIT = 416
ROW_NS, HOP_NS, HANDLER_NS, RELAY_NS = 5.6, 1900.0, 80.0, 1500.0
QUEUE_NS = {"x": 5500.0, "y": 3500.0, "z": 4500.0}
LARGE_NS, BLOCK_NS, SMALL_NS, PAIR_NS, SINGLE_NS = 170.0, 145.0, 460.0, 740.0, 0.0
Z_RANK, Y_RANK = (2, 0.5, -2, 0), (0.5, -0.5, 1, -1)
HALVES = {1: (None,), 2: (None,)}
GROUPS = (4, 2, 2)
EARLY, LATER = (0, 1, -1, 2, -2), (3, -3, 4)
TOGETHER = 2
LATE = 24
VMEM_KIB = 48 * 2**10


def part_rows(part, half):
    start, rows = (0, SPLIT) if part == 1 else (SPLIT, ROWS - SPLIT)
    if half is None:
        return start, rows
    cut = rows // 2 // 16 * 16
    return (start, cut) if half == 0 else (start + cut, rows - cut)


def group_of(block):
    first = 0
    for g, size in enumerate(GROUPS):
        if block < first + size:
            return g, block - first
        first += size


def plan():
    free, ready, heap, count = collections.defaultdict(float), collections.defaultdict(list), [], itertools.count()
    steps, now = [], 0.0
    large = [(g, dz % NZ) for dz in EARLY for g in range(len(GROUPS))]
    small = [(dz % NZ, dy) for dz in LATER for dy in (0, 1, 3, 2)]
    rows_left = {(dz, dy): ROWS for dz in range(NZ) for dy in range(NY)}
    rows_left[0, 0] = 0
    blocks_left, blocks_at = [4 * size for size in GROUPS], [0.0] * len(GROUPS)

    def side(direction):
        return 0 if direction > 0 else 1

    def add(part, dz, dy, half, axis, direction):
        dz, dy = (dz - direction, dy) if axis == "z" else (dz, dy - direction)
        weights = Z_RANK if axis == "z" else Y_RANK
        rank = sum(w * v for w, v in zip(weights, (abs(dz), abs(dy), part == 2, half is not None)))
        piece = ("i", part, dz, dy, half, axis, direction)
        ready[axis, direction].append((rank, next(count), part_rows(part, half)[1], piece))

    def add_block(block, stage, direction):
        rank = block if stage == 2 else NB + block
        rows = SLOTS * 16 // stage
        ready["x", direction].append((rank, next(count), rows, ("a", block, stage, direction)))

    def sends():
        out, more = [], True
        while more:
            more = False
            for link in [(axis, direction) for axis in "yzx" for direction in (1, -1)]:
                if ready[link] and free[link] - now < QUEUE_NS[link[0]]:
                    item = min(ready[link])
                    ready[link].remove(item)
                    free[link] = max(now, free[link]) + item[2] * ROW_NS
                    heapq.heappush(heap, (free[link] + HOP_NS, next(count), item[3]))
                    out.append(item[3])
                    more = True
        return out

    for direction in (1, -1):
        for part in (1, 2):
            for half in HALVES[part]:
                add(part, 0, 0, half, "y", direction)
                add(part, 0, 0, half, "z", direction)
        for block in range(NB):
            add_block(block, 1, direction)
    steps.append((None, sends()))
    while heap or small:
        while small and (not heap or heap[0][0] > now):
            able = [g for g in range(len(GROUPS)) if not blocks_left[g] and (blocks_at[g] <= now or not heap)]
            fit = [u for u in large if u[0] in able and not any(rows_left[u[1], dy] for dy in range(NY))]
            if fit:
                large.remove(fit[0])
                now = max(now, blocks_at[fit[0][0]]) + LARGE_NS + BLOCK_NS * GROUPS[fit[0][0]]
                steps.append((("large", *fit[0]), sends()))
                continue
            fit = [u for u in small if len(able) == len(GROUPS) and not rows_left[u]]
            if not fit:
                break
            if len(fit) == 1 and len(small) > 1 and heap and heap[0][0] < now + SINGLE_NS:
                break
            fit = fit[:TOGETHER]
            small = [u for u in small if u not in fit]
            now += SMALL_NS if len(fit) == 1 else PAIR_NS
            steps.append((("small", *fit), sends()))
        if not heap:
            continue
        at, _, piece = heapq.heappop(heap)
        now = max(now, at) + HANDLER_NS
        if piece[0] == "a":
            _, block, stage, direction = piece
            if stage == 1:
                add_block(block, 2, direction)
            g = group_of(block)[0]
            blocks_left[g] -= 1
            blocks_at[g] = now + RELAY_NS
        else:
            _, part, dz, dy, half, axis, direction = piece
            rows_left[dz % NZ, dy % NY] -= part_rows(part, half)[1]
            hops, last = (abs(dz), NZ // 2) if axis == "z" else (abs(dy), NY // 2)
            if hops < last - 1:
                add(part, dz, dy, half, axis, direction)
            elif hops == last - 1 and half in (None, side(direction)):
                add(part, dz, dy, side(direction), axis, direction)
            if (part, axis) in ((1, "y"), (2, "z")):
                for turn in (1, -1):
                    add(part, dz, dy, half, "z" if axis == "y" else "y", turn)
        steps.append((piece, sends()))
    return steps


def kernel(steps, amp, ints, tiles_hbm, counts_hbm, total, last_left, last_right, blocks0, blocks1, blocks2, pieces, tiles, counts, slot_v,
           slot_s, send_sem, recv_sem, relay_send, relay_recv, local_sem):
    occ, vir = lax.axis_index("occ"), lax.axis_index("vir")
    x, core, z, y = vir // 2, vir % 2, occ // NY, occ % NY
    blocks = (blocks0, blocks1, blocks2)

    def near(axis, d):
        if axis == "x":
            return {"vir": (x + d + NX) % NX * 2 + core}
        if axis == "y":
            return {"occ": z * NY + (y + d + NY) % NY}
        return {"occ": (z + d + NZ) % NZ * NY + y}

    partner = {"vir": x * 2 + 1 - core}
    barrier = pltpu.get_barrier_semaphore()
    for device in [near(axis, d) for axis in "zyx" for d in (1, -1)] + [partner]:
        pl.semaphore_signal(barrier, inc=1, device_id=device, device_id_type=MESH)
    pl.semaphore_wait(barrier, 7)

    def vir_at(d, c):
        return (x + d + NX) % NX * 2 + c

    def block_at(owner, b, half=None):
        slots = pl.ds(0, SLOTS) if half is None else pl.ds(half * (SLOTS // 2), SLOTS // 2)
        g, place = group_of(b)
        return blocks[g].at[owner, place, slots]

    def side(d):
        return 0 if d > 0 else 1

    order = [piece for _, sent in steps for piece in sent]
    number = {piece: i for i, piece in enumerate(order)}

    def copy(piece, arriving=False):
        i = number[piece]
        if piece[0] == "a":
            _, b, stage, d = piece
            axis = "x"
            if stage == 1:
                src, dst = amp.at[b], block_at(vir_at(-d, core) if arriving else vir, b)
            else:
                src = block_at(vir_at(-d, core), b, side(d))
                dst = block_at(vir_at(2, core), b, side(d)) if arriving else src
        else:
            _, part, dz, dy, half, axis, d = piece
            rows = pl.ds(*part_rows(part, half))
            oz, oy = (dz + d, dy) if axis == "z" else (dz, dy + d)
            src = ints.at[rows] if (oz, oy) == (0, 0) else pieces.at[oz % NZ, oy % NY, rows]
            dst = pieces.at[dz % NZ, dy % NY, rows]
        return pltpu.make_async_remote_copy(
            src, dst, send_sem.at[i], recv_sem.at[i], device_id=near(axis, d), device_id_type=MESH
        )

    relays = [("own", b) for b in range(NB)] + [piece for piece in order if piece[0] == "a"]
    relay_number = {piece: i for i, piece in enumerate(relays)}

    def relay(piece, arriving=False):
        i = relay_number[piece]
        c = 1 - core if arriving else core
        if piece[0] == "own":
            dst = block_at(vir_at(0, c), piece[1])
            src = amp.at[piece[1]]
        else:
            _, b, stage, d = piece
            dst = block_at(vir_at(-d, c), b) if stage == 1 else block_at(vir_at(2, c), b, side(d))
            src = dst
        return pltpu.make_async_remote_copy(
            src, dst, relay_send.at[i], relay_recv.at[i], device_id=partner, device_id_type=MESH
        )

    own_blocks = [pltpu.make_async_copy(amp.at[b], block_at(vir, b), local_sem.at[b]) for b in range(NB)]
    own_piece = pltpu.make_async_copy(ints, pieces.at[0, 0], local_sem.at[NB])

    def prepare():
        lists = [
            pltpu.make_async_copy(tiles_hbm, tiles, local_sem.at[NB + 4]),
            pltpu.make_async_copy(counts_hbm, counts, local_sem.at[NB + 5]),
        ]
        for read in lists:
            read.start()
        own_piece.start()
        for b in range(NB):
            own_blocks[b].start()
            relay(("own", b)).start()
        for read in lists:
            read.wait()
        lane = lax.broadcasted_iota(jnp.int32, (NB, 128), 1)
        row = lax.broadcasted_iota(jnp.int32, (NB, 128), 0)
        tile = 2 * ((z + lane // 8) % NZ * NY + (y + lane // 2 % 4) % NY) + lane % 2
        live = jnp.zeros((NB, 128), jnp.int32)
        for b in range(NB):
            live = jnp.where(row == b, counts[b], live)
        slot = jnp.full((NB, 128), SLOTS, jnp.int32)
        listed = tiles[...]
        for s in range(SLOTS):
            slot = jnp.where((listed[:, s : s + 1] == tile) & (live > s), s, slot)
        slot_v[...] = slot
        to_scalars = pltpu.make_async_copy(slot_v, slot_s, local_sem.at[NB + 1])
        to_scalars.start()
        for group, size in zip(blocks, GROUPS):
            group[:, :, SLOTS] = jnp.zeros((2 * NX, size, 16, TILE), jnp.bfloat16)
        total[...] = jnp.zeros_like(total)
        to_scalars.wait()

    def group_ready(g):
        for b in range(NB):
            if group_of(b)[0] == g:
                own_blocks[b].wait()
        for piece in relays:
            if group_of(piece[1])[0] == g:
                relay(piece, True).wait_recv()

    rounds, units = [[]], []
    for event, sent in steps:
        if event is not None and event[0] in ("large", "small"):
            units.append(event)
            rounds.append([])
            event = None
        rounds[-1].append((event, sent))
    first_use = [[u[:2] for u in units].index(("large", g)) for g in range(len(GROUPS))]

    def run_round(r):
        for i, (event, sent) in enumerate(rounds[r]):
            if event is not None:
                copy(event, True).wait_recv()
            for piece in sent:
                copy(piece).start()
            if event is not None and event[0] == "a":
                relay(event).start()
            if r == 0 and i == 0:
                prepare()
        if r == 0:
            own_piece.wait()
        for g in range(len(GROUPS)):
            if r == first_use[g]:
                group_ready(g)

    def gather(b, dz, tiles):
        g, place = group_of(b)
        found = [slot_s[b, dz * 8 + q] for q in tiles]
        return jnp.concatenate([blocks[g][:, place, s].reshape(TILE, TILE) for s in found], axis=1)

    def origin(dz, dy):
        return jnp.concatenate(
            [
                jnp.concatenate([pieces[dz, dy, pl.ds((j * NA + a) * TILE, TILE)] for a in range(NA)], axis=1)
                for j in range(2)
            ],
            axis=0,
        )

    def run_large(g, dz):
        mine = [b for b in range(NB) if group_of(b)[0] == g]
        left = jnp.concatenate([gather(b, dz, range(8)) for b in mine], axis=0)
        right = jnp.concatenate([origin(dz, dy) for dy in range(NY)], axis=0)
        here = pl.ds(mine[0] * TILE, len(mine) * TILE)
        total[here] += jnp.dot(left, right, preferred_element_type=jnp.float32)

    def left_of(origins):
        return jnp.concatenate(
            [
                jnp.concatenate([gather(b, dz, (2 * dy, 2 * dy + 1)) for b in range(NB)], axis=0)
                for dz, dy in origins
            ],
            axis=1,
        )

    def right_of(origins):
        return jnp.concatenate([origin(dz, dy) for dz, dy in origins], axis=0)

    def run_small(*origins):
        return total[...] + jnp.dot(left_of(origins), right_of(origins), preferred_element_type=jnp.float32)

    def run_units(first, stop):
        @pl.loop(first, stop)
        def _(u):
            dz = jnp.int32(0)
            for r in range(first, stop):
                pl.when(u == r)(functools.partial(run_round, r))
                dz = jnp.where(u == r, units[r][2], dz)
            run_large(units[first][1], dz)

    u = 0
    while u < len(units) - 1:
        if units[u][0] == "small":
            run_round(u)
            total[...] = run_small(*units[u][1:])
            u += 1
            continue
        stop = u + 1
        while units[stop][:2] == units[u][:2]:
            stop += 1
        run_units(u, stop)
        u = stop

    for piece in order[:-LATE]:
        copy(piece).wait_send()
    for piece in relays:
        relay(piece).wait_send()
    last_left[...] = left_of(units[-1][1:])
    run_round(len(units) - 1)
    last_right[...] = right_of(units[-1][1:])
    for piece in order[-LATE:]:
        copy(piece).wait_send()


def write_out(sums, left, right, out, rounded, sems):
    writes = []
    for first in range(0, NB, 2):
        rows = pl.ds(first * TILE, 2 * TILE)
        chunk = sums[rows] + jnp.dot(left[rows], right[...], preferred_element_type=jnp.float32)
        for b in range(2):
            for a in range(NA):
                tile = chunk[b * TILE : (b + 1) * TILE, a * TILE : (a + 1) * TILE]
                rounded[first + b, a] = tile.astype(jnp.bfloat16)
        here = pl.ds(first, 2)
        writes.append(pltpu.make_async_copy(rounded.at[here], out.at[here], sems.at[first]))
        writes[-1].start()
    for write in writes:
        write.wait()


def on_device(amplitudes, integrals, tile_list, counts):
    steps = plan()
    depth = 2 * TILE * (len([e for e, _ in steps if e is not None and e[0] == "small"][-1]) - 1)
    operands = (amplitudes, integrals.reshape(ROWS, TILE), tile_list, counts)
    copies = sum(len(sent) for _, sent in steps)
    parts = pl.pallas_call(
        functools.partial(kernel, steps),
        out_shape=[
            pltpu.VMEM((NB * TILE, NA * TILE), jnp.float32),
            pltpu.VMEM((NB * TILE, depth), jnp.bfloat16),
            pltpu.VMEM((depth, NA * TILE), jnp.bfloat16),
        ],
        in_specs=[pl.BlockSpec(memory_space=pltpu.HBM)] * 4,
        out_specs=[pl.BlockSpec(memory_space=pltpu.VMEM)] * 3,
        scratch_shapes=[
            *[pltpu.VMEM((2 * NX, size, SLOTS + 1, 16, TILE), jnp.bfloat16) for size in GROUPS],
            pltpu.VMEM((NZ, NY, ROWS, TILE), jnp.bfloat16),
            pltpu.VMEM((NB, SLOTS), jnp.int32),
            pltpu.SMEM((NB,), jnp.int32),
            pltpu.VMEM((NB, 128), jnp.int32),
            pltpu.SMEM((NB, 128), jnp.int32),
            pltpu.SemaphoreType.DMA((copies,)),
            pltpu.SemaphoreType.DMA((copies,)),
            pltpu.SemaphoreType.DMA((5 * NB,)),
            pltpu.SemaphoreType.DMA((5 * NB,)),
            pltpu.SemaphoreType.DMA((NB + 6,)),
        ],
        compiler_params=pltpu.CompilerParams(
            collective_id=0, has_side_effects=True, vmem_limit_bytes=VMEM_KIB * 2**10
        ),
    )(*[pltpu.with_memory_space_constraint(x, pltpu.HBM) for x in operands])
    return pl.pallas_call(
        write_out,
        out_shape=pltpu.HBM((NB, NA, TILE, TILE), jnp.bfloat16),
        in_specs=[pl.BlockSpec(memory_space=pltpu.VMEM)] * 3,
        out_specs=pl.BlockSpec(memory_space=pl.ANY),
        scratch_shapes=[pltpu.VMEM((NB, NA, TILE, TILE), jnp.bfloat16), pltpu.SemaphoreType.DMA((NB,))],
    )(*[pltpu.with_memory_space_constraint(x, pltpu.VMEM) for x in parts])


def solution(mesh):
    placed = (P("occ", None, "vir", None), P("occ", "vir", None, None), P("occ", None), P("occ"))
    return jax.shard_map(
        on_device,
        mesh=mesh,
        in_specs=placed,
        out_specs=P("occ", "vir", None, None),
        check_vma=False,
    )
```

```python
import collections
import functools
import heapq
import itertools

import jax
import jax.numpy as jnp
from jax import lax
from jax.experimental import pallas as pl
from jax.experimental.pallas import tpu as pltpu
from jax.sharding import PartitionSpec as P

MESH = pl.DeviceIdType.MESH
NX, NY, NZ = 4, 4, 8
TILE, SLOTS, NB, NA = 128, 32, 8, 4
ROWS = 2 * NA * TILE
SPLIT = 416
ROW_NS, HOP_NS, HANDLER_NS, RELAY_NS = 5.6, 1900.0, 80.0, 1500.0
QUEUE_NS = {"x": 5500.0, "y": 3500.0, "z": 4500.0}
LARGE_NS, BLOCK_NS, SMALL_NS, PAIR_NS, SINGLE_NS = 170.0, 145.0, 460.0, 740.0, 0.0
Z_RANK, Y_RANK = (2, 0.5, -2, 0), (0.5, -0.5, 1, -1)
HALVES = {1: (None,), 2: (None,)}
GROUPS = (4, 2, 2)
EARLY, LATER = (0, 1, -1, 2, -2), (3, -3, 4)
TOGETHER = 2
LATE = 24
VMEM_KIB = 48 * 2**10


def part_rows(part, half):
    start, rows = (0, SPLIT) if part == 1 else (SPLIT, ROWS - SPLIT)
    if half is None:
        return start, rows
    cut = rows // 2 // 16 * 16
    return (start, cut) if half == 0 else (start + cut, rows - cut)


def group_of(block):
    first = 0
    for g, size in enumerate(GROUPS):
        if block < first + size:
            return g, block - first
        first += size


def plan():
    free, ready, heap, count = collections.defaultdict(float), collections.defaultdict(list), [], itertools.count()
    steps, now = [], 0.0
    large = [(g, dz % NZ) for dz in EARLY for g in range(len(GROUPS))]
    small = [(dz % NZ, dy) for dz in LATER for dy in (0, 1, 3, 2)]
    rows_left = {(dz, dy): ROWS for dz in range(NZ) for dy in range(NY)}
    rows_left[0, 0] = 0
    blocks_left, blocks_at = [4 * size for size in GROUPS], [0.0] * len(GROUPS)

    def side(direction):
        return 0 if direction > 0 else 1

    def add(part, dz, dy, half, axis, direction):
        dz, dy = (dz - direction, dy) if axis == "z" else (dz, dy - direction)
        weights = Z_RANK if axis == "z" else Y_RANK
        rank = sum(w * v for w, v in zip(weights, (abs(dz), abs(dy), part == 2, half is not None)))
        piece = ("i", part, dz, dy, half, axis, direction)
        ready[axis, direction].append((rank, next(count), part_rows(part, half)[1], piece))

    def add_block(block, stage, direction):
        rank = block if stage == 2 else NB + block
        rows = SLOTS * 16 // stage
        ready["x", direction].append((rank, next(count), rows, ("a", block, stage, direction)))

    def sends():
        out, more = [], True
        while more:
            more = False
            for link in [(axis, direction) for axis in "yzx" for direction in (1, -1)]:
                if ready[link] and free[link] - now < QUEUE_NS[link[0]]:
                    item = min(ready[link])
                    ready[link].remove(item)
                    free[link] = max(now, free[link]) + item[2] * ROW_NS
                    heapq.heappush(heap, (free[link] + HOP_NS, next(count), item[3]))
                    out.append(item[3])
                    more = True
        return out

    for direction in (1, -1):
        for part in (1, 2):
            for half in HALVES[part]:
                add(part, 0, 0, half, "y", direction)
                add(part, 0, 0, half, "z", direction)
        for block in range(NB):
            add_block(block, 1, direction)
    steps.append((None, sends()))
    while heap or small:
        while small and (not heap or heap[0][0] > now):
            able = [g for g in range(len(GROUPS)) if not blocks_left[g] and (blocks_at[g] <= now or not heap)]
            fit = [u for u in large if u[0] in able and not any(rows_left[u[1], dy] for dy in range(NY))]
            if fit:
                large.remove(fit[0])
                now = max(now, blocks_at[fit[0][0]]) + LARGE_NS + BLOCK_NS * GROUPS[fit[0][0]]
                steps.append((("large", *fit[0]), sends()))
                continue
            fit = [u for u in small if len(able) == len(GROUPS) and not rows_left[u]]
            if not fit:
                break
            if len(fit) == 1 and len(small) > 1 and heap and heap[0][0] < now + SINGLE_NS:
                break
            fit = fit[:TOGETHER]
            small = [u for u in small if u not in fit]
            now += SMALL_NS if len(fit) == 1 else PAIR_NS
            steps.append((("small", *fit), sends()))
        if not heap:
            continue
        at, _, piece = heapq.heappop(heap)
        now = max(now, at) + HANDLER_NS
        if piece[0] == "a":
            _, block, stage, direction = piece
            if stage == 1:
                add_block(block, 2, direction)
            g = group_of(block)[0]
            blocks_left[g] -= 1
            blocks_at[g] = now + RELAY_NS
        else:
            _, part, dz, dy, half, axis, direction = piece
            rows_left[dz % NZ, dy % NY] -= part_rows(part, half)[1]
            hops, last = (abs(dz), NZ // 2) if axis == "z" else (abs(dy), NY // 2)
            if hops < last - 1:
                add(part, dz, dy, half, axis, direction)
            elif hops == last - 1 and half in (None, side(direction)):
                add(part, dz, dy, side(direction), axis, direction)
            if (part, axis) in ((1, "y"), (2, "z")):
                for turn in (1, -1):
                    add(part, dz, dy, half, "z" if axis == "y" else "y", turn)
        steps.append((piece, sends()))
    return steps


def kernel(steps, amp, ints, tiles_hbm, counts_hbm, total, last_left, last_right, blocks0, blocks1, blocks2, pieces, tiles, counts, slot_v,
           slot_s, send_sem, recv_sem, relay_send, relay_recv, local_sem):
    occ, vir = lax.axis_index("occ"), lax.axis_index("vir")
    x, core, z, y = vir // 2, vir % 2, occ // NY, occ % NY
    blocks = (blocks0, blocks1, blocks2)

    def near(axis, d):
        if axis == "x":
            return {"vir": (x + d + NX) % NX * 2 + core}
        if axis == "y":
            return {"occ": z * NY + (y + d + NY) % NY}
        return {"occ": (z + d + NZ) % NZ * NY + y}

    partner = {"vir": x * 2 + 1 - core}
    barrier = pltpu.get_barrier_semaphore()
    for device in [near(axis, d) for axis in "zyx" for d in (1, -1)] + [partner]:
        pl.semaphore_signal(barrier, inc=1, device_id=device, device_id_type=MESH)
    pl.semaphore_wait(barrier, 7)

    def vir_at(d, c):
        return (x + d + NX) % NX * 2 + c

    def block_at(owner, b, half=None):
        slots = pl.ds(0, SLOTS) if half is None else pl.ds(half * (SLOTS // 2), SLOTS // 2)
        g, place = group_of(b)
        return blocks[g].at[owner, place, slots]

    def side(d):
        return 0 if d > 0 else 1

    order = [piece for _, sent in steps for piece in sent]
    number = {piece: i for i, piece in enumerate(order)}

    def copy(piece, arriving=False):
        i = number[piece]
        if piece[0] == "a":
            _, b, stage, d = piece
            axis = "x"
            if stage == 1:
                src, dst = amp.at[b], block_at(vir_at(-d, core) if arriving else vir, b)
            else:
                src = block_at(vir_at(-d, core), b, side(d))
                dst = block_at(vir_at(2, core), b, side(d)) if arriving else src
        else:
            _, part, dz, dy, half, axis, d = piece
            rows = pl.ds(*part_rows(part, half))
            oz, oy = (dz + d, dy) if axis == "z" else (dz, dy + d)
            src = ints.at[rows] if (oz, oy) == (0, 0) else pieces.at[oz % NZ, oy % NY, rows]
            dst = pieces.at[dz % NZ, dy % NY, rows]
        return pltpu.make_async_remote_copy(
            src, dst, send_sem.at[i], recv_sem.at[i], device_id=near(axis, d), device_id_type=MESH
        )

    relays = [("own", b) for b in range(NB)] + [piece for piece in order if piece[0] == "a"]
    relay_number = {piece: i for i, piece in enumerate(relays)}

    def relay(piece, arriving=False):
        i = relay_number[piece]
        c = 1 - core if arriving else core
        if piece[0] == "own":
            dst = block_at(vir_at(0, c), piece[1])
            src = amp.at[piece[1]]
        else:
            _, b, stage, d = piece
            dst = block_at(vir_at(-d, c), b) if stage == 1 else block_at(vir_at(2, c), b, side(d))
            src = dst
        return pltpu.make_async_remote_copy(
            src, dst, relay_send.at[i], relay_recv.at[i], device_id=partner, device_id_type=MESH
        )

    own_blocks = [pltpu.make_async_copy(amp.at[b], block_at(vir, b), local_sem.at[b]) for b in range(NB)]
    own_piece = pltpu.make_async_copy(ints, pieces.at[0, 0], local_sem.at[NB])

    def prepare():
        lists = [
            pltpu.make_async_copy(tiles_hbm, tiles, local_sem.at[NB + 4]),
            pltpu.make_async_copy(counts_hbm, counts, local_sem.at[NB + 5]),
        ]
        for read in lists:
            read.start()
        own_piece.start()
        for b in range(NB):
            own_blocks[b].start()
            relay(("own", b)).start()
        for read in lists:
            read.wait()
        lane = lax.broadcasted_iota(jnp.int32, (NB, 128), 1)
        row = lax.broadcasted_iota(jnp.int32, (NB, 128), 0)
        tile = 2 * ((z + lane // 8) % NZ * NY + (y + lane // 2 % 4) % NY) + lane % 2
        live = jnp.zeros((NB, 128), jnp.int32)
        for b in range(NB):
            live = jnp.where(row == b, counts[b], live)
        slot = jnp.full((NB, 128), SLOTS, jnp.int32)
        listed = tiles[...]
        for s in range(SLOTS):
            slot = jnp.where((listed[:, s : s + 1] == tile) & (live > s), s, slot)
        slot_v[...] = slot
        to_scalars = pltpu.make_async_copy(slot_v, slot_s, local_sem.at[NB + 1])
        to_scalars.start()
        for group, size in zip(blocks, GROUPS):
            group[:, :, SLOTS] = jnp.zeros((2 * NX, size, 16, TILE), jnp.bfloat16)
        total[...] = jnp.zeros_like(total)
        to_scalars.wait()

    def group_ready(g):
        for b in range(NB):
            if group_of(b)[0] == g:
                own_blocks[b].wait()
        for piece in relays:
            if group_of(piece[1])[0] == g:
                relay(piece, True).wait_recv()

    rounds, units = [[]], []
    for event, sent in steps:
        if event is not None and event[0] in ("large", "small"):
            units.append(event)
            rounds.append([])
            event = None
        rounds[-1].append((event, sent))
    first_use = [[u[:2] for u in units].index(("large", g)) for g in range(len(GROUPS))]

    def run_round(r):
        for i, (event, sent) in enumerate(rounds[r]):
            if event is not None:
                copy(event, True).wait_recv()
            for piece in sent:
                copy(piece).start()
            if event is not None and event[0] == "a":
                relay(event).start()
            if r == 0 and i == 0:
                prepare()
        if r == 0:
            own_piece.wait()
        for g in range(len(GROUPS)):
            if r == first_use[g]:
                group_ready(g)

    def gather(b, dz, tiles):
        g, place = group_of(b)
        found = [slot_s[b, dz * 8 + q] for q in tiles]
        return jnp.concatenate([blocks[g][:, place, s].reshape(TILE, TILE) for s in found], axis=1)

    def origin(dz, dy):
        return jnp.concatenate(
            [
                jnp.concatenate([pieces[dz, dy, pl.ds((j * NA + a) * TILE, TILE)] for a in range(NA)], axis=1)
                for j in range(2)
            ],
            axis=0,
        )

    def run_large(g, dz):
        mine = [b for b in range(NB) if group_of(b)[0] == g]
        left = jnp.concatenate([gather(b, dz, range(8)) for b in mine], axis=0)
        right = jnp.concatenate([origin(dz, dy) for dy in range(NY)], axis=0)
        here = pl.ds(mine[0] * TILE, len(mine) * TILE)
        total[here] += jnp.dot(left, right, preferred_element_type=jnp.float32)

    def left_of(origins):
        return jnp.concatenate(
            [
                jnp.concatenate([gather(b, dz, (2 * dy, 2 * dy + 1)) for b in range(NB)], axis=0)
                for dz, dy in origins
            ],
            axis=1,
        )

    def right_of(origins):
        return jnp.concatenate([origin(dz, dy) for dz, dy in origins], axis=0)

    def run_small(*origins):
        return total[...] + jnp.dot(left_of(origins), right_of(origins), preferred_element_type=jnp.float32)

    def run_units(first, stop):
        @pl.loop(first, stop)
        def _(u):
            dz = jnp.int32(0)
            for r in range(first, stop):
                pl.when(u == r)(functools.partial(run_round, r))
                dz = jnp.where(u == r, units[r][2], dz)
            run_large(units[first][1], dz)

    u = 0
    while u < len(units) - 1:
        if units[u][0] == "small":
            run_round(u)
            total[...] = run_small(*units[u][1:])
            u += 1
            continue
        stop = u + 1
        while units[stop][:2] == units[u][:2]:
            stop += 1
        run_units(u, stop)
        u = stop

    for piece in order[:-LATE]:
        copy(piece).wait_send()
    for piece in relays:
        relay(piece).wait_send()
    last_left[...] = left_of(units[-1][1:])
    run_round(len(units) - 1)
    last_right[...] = right_of(units[-1][1:])
    for piece in order[-LATE:]:
        copy(piece).wait_send()


def write_out(sums, left, right, out, rounded, sems):
    writes = []
    for first, size in ((0, 1), (1, 2), (3, 2), (5, 2), (7, 1)):
        rows = pl.ds(first * TILE, size * TILE)
        chunk = sums[rows] + jnp.dot(left[rows], right[...], preferred_element_type=jnp.float32)
        for b in range(size):
            for a in range(NA):
                tile = chunk[b * TILE : (b + 1) * TILE, a * TILE : (a + 1) * TILE]
                rounded[first + b, a] = tile.astype(jnp.bfloat16)
        here = pl.ds(first, size)
        writes.append(pltpu.make_async_copy(rounded.at[here], out.at[here], sems.at[first]))
        writes[-1].start()
    for write in writes:
        write.wait()


def on_device(amplitudes, integrals, tile_list, counts):
    steps = plan()
    depth = 2 * TILE * (len([e for e, _ in steps if e is not None and e[0] == "small"][-1]) - 1)
    operands = (amplitudes, integrals.reshape(ROWS, TILE), tile_list, counts)
    copies = sum(len(sent) for _, sent in steps)
    parts = pl.pallas_call(
        functools.partial(kernel, steps),
        out_shape=[
            pltpu.VMEM((NB * TILE, NA * TILE), jnp.float32),
            pltpu.VMEM((NB * TILE, depth), jnp.bfloat16),
            pltpu.VMEM((depth, NA * TILE), jnp.bfloat16),
        ],
        in_specs=[pl.BlockSpec(memory_space=pltpu.HBM)] * 4,
        out_specs=[pl.BlockSpec(memory_space=pltpu.VMEM)] * 3,
        scratch_shapes=[
            *[pltpu.VMEM((2 * NX, size, SLOTS + 1, 16, TILE), jnp.bfloat16) for size in GROUPS],
            pltpu.VMEM((NZ, NY, ROWS, TILE), jnp.bfloat16),
            pltpu.VMEM((NB, SLOTS), jnp.int32),
            pltpu.SMEM((NB,), jnp.int32),
            pltpu.VMEM((NB, 128), jnp.int32),
            pltpu.SMEM((NB, 128), jnp.int32),
            pltpu.SemaphoreType.DMA((copies,)),
            pltpu.SemaphoreType.DMA((copies,)),
            pltpu.SemaphoreType.DMA((5 * NB,)),
            pltpu.SemaphoreType.DMA((5 * NB,)),
            pltpu.SemaphoreType.DMA((NB + 6,)),
        ],
        compiler_params=pltpu.CompilerParams(
            collective_id=0, has_side_effects=True, vmem_limit_bytes=VMEM_KIB * 2**10
        ),
    )(*[pltpu.with_memory_space_constraint(x, pltpu.HBM) for x in operands])
    return pl.pallas_call(
        write_out,
        out_shape=pltpu.HBM((NB, NA, TILE, TILE), jnp.bfloat16),
        in_specs=[pl.BlockSpec(memory_space=pltpu.VMEM)] * 3,
        out_specs=pl.BlockSpec(memory_space=pl.ANY),
        scratch_shapes=[pltpu.VMEM((NB, NA, TILE, TILE), jnp.bfloat16), pltpu.SemaphoreType.DMA((NB,))],
    )(*[pltpu.with_memory_space_constraint(x, pltpu.VMEM) for x in parts])


def solution(mesh):
    placed = (P("occ", None, "vir", None), P("occ", "vir", None, None), P("occ", None), P("occ"))
    return jax.shard_map(
        on_device,
        mesh=mesh,
        in_specs=placed,
        out_specs=P("occ", "vir", None, None),
        check_vma=False,
    )
```
